32 devices in a mesh: dp: 8 (over z, y), group: 4 (over x, core).
Axes of the slice: x: 2, y: 2, z: 4, core: 2. Of those that a mesh axis runs over, the one named last changes fastest.
Arguments:
- gradients: bfloat16 [32, 2, 2048, 512], P(('dp', 'group'))
- errors: float32 [32, 2, 2048, 512], P(('dp', 'group')), may hold values from -4 to 4
- warm_right: float32 [2, 512, 32], replicated, may hold values from -6 to 6
- norm_grads: float32 [32, 2, 2048], P(('dp', 'group'))
- norm_weights: float32 [2, 2048], replicated, may hold values from 0.5 to 1.5
- norm_moment: float32 [2, 2048], replicated, may hold values from -4 to 4
- owners: int32 [32], replicated, may hold values from 0 to 31, as said below
- slot_weights: bfloat16 [32, 2, 128, 512], P(('dp', 'group')), may hold values from -6 to 6
- slot_moment: float32 [32, 2, 128, 512], P(('dp', 'group')), may hold values from -4 to 4
Outputs:
- new_errors: float32 [32, 2, 2048, 512], P(('dp', 'group'))
- new_slot_moment: float32 [32, 2, 128, 512], P(('dp', 'group'))
- new_weights: bfloat16 [2, 2048, 512], replicated
- new_norm_weights: float32 [2, 2048], replicated
- new_norm_moment: float32 [2, 2048], replicated
The draws below stay inside these ranges and needn't reach their ends.
Inputs may be any that keep to these rules, and one draw needn't show every extreme that they name: `owners`: each replica owns at most 2 pieces and some replica owns exactly 2; a replica's pieces occupy its slots in increasing piece order, the other slots hold nothing that is read.
All inputs are finite; a program needn't handle non-finite values.
Results may differ from the reference program's by a relative error of at most 0.0004.
Values may be sent and summed in bfloat16 or wider, within the bound.
A program may use at most 128 MiB of HBM per device.

```python
import jax
import jax.numpy as jnp
from jax import lax

DW = 2048
KV = 512
RANK = 32
SLOTS = 2
REPLICAS = 32
PIECES = 32
RB = 128


def draw_gradients(key, part):
    own_key = jax.random.fold_in(key, 12)
    own = jax.random.normal(own_key, (REPLICAS, 2, DW, KV), jnp.float32)
    values = own
    return jnp.clip(values, -12.0, 12.0).astype(jnp.bfloat16)


def draw_norm_grads(key, part):
    common_key = jax.random.fold_in(key, 21)
    own_key = jax.random.fold_in(key, 22)
    steps = jnp.arange(REPLICAS).astype(jnp.float32) / max(REPLICAS - 1, 1)
    rise = 1.0 + 2.0 * steps
    common = 2.0 * jax.random.normal(common_key, (2, DW), jnp.float32)
    own = 2.0 * jax.random.normal(own_key, (REPLICAS, 2, DW), jnp.float32)
    return jnp.clip(common[None] + own * rise[:, None, None], -40.0, 40.0)


def draw_owners(key, part):
    first_key = jax.random.fold_in(key, 31)
    rest_key = jax.random.fold_in(key, 32)
    order_key = jax.random.fold_in(key, 33)
    full_owner = jax.random.randint(first_key, (), 0, REPLICAS).astype(jnp.int32)
    rest = (jax.random.permutation(rest_key, (REPLICAS - 1) * SLOTS)[:PIECES - SLOTS] // SLOTS).astype(jnp.int32)
    rest = rest + (rest >= full_owner).astype(jnp.int32)
    owners_all = jnp.concatenate([full_owner * jnp.ones((SLOTS,), jnp.int32), rest])
    order = jax.random.permutation(order_key, PIECES)
    return owners_all[order].astype(jnp.int32)


def block_scale(key, dims, shards, least, high):
    loudness = 1.0
    for position, parts in shards:
        draws = jax.random.uniform(jax.random.fold_in(jax.random.fold_in(key, 6), position), (parts,), jnp.float32, least / len(shards), high / len(shards))
        loudness = loudness * jnp.repeat(jnp.exp(draws), dims[position] // parts).reshape((-1,) + (1,) * (len(dims) - 1 - position))
    return loudness


def noise(stream_key, extent, spread, most, shards=(), kind=jnp.bfloat16):
    values = jax.random.normal(stream_key, extent, jnp.float32) * spread
    if len(shards) > 0:
        values = block_scale(stream_key, extent, shards, -0.22, 0.18) * values
    return jnp.clip(values, min=-most, max=most).astype(kind)


def setup_inputs(seed: int = 0) -> dict:
    splits = jax.random.split(jax.random.key(seed), 10)
    return {
        "gradients": draw_gradients(jax.random.fold_in(splits[9], 71), 0),
        "errors": noise(splits[1], (REPLICAS, 2, DW, KV), 0.5, 4.0, ((0, 32),), jnp.float32),
        "warm_right": noise(splits[2], (2, KV, RANK), 1.0, 6.0, (), jnp.float32),
        "norm_grads": draw_norm_grads(jax.random.fold_in(splits[9], 71), 0),
        "norm_weights": jnp.clip(1.0 + 0.1 * jax.random.normal(splits[4], (2, DW), jnp.float32), 0.5, 1.5),
        "norm_moment": noise(splits[5], (2, DW), 0.5, 4.0, (), jnp.float32),
        "owners": draw_owners(jax.random.fold_in(splits[9], 71), 0),
        "slot_weights": noise(splits[7], (REPLICAS, SLOTS, RB, KV), 1.0, 6.0, ((0, 32),)),
        "slot_moment": noise(splits[8], (REPLICAS, SLOTS, RB, KV), 0.5, 4.0, ((0, 32),), jnp.float32),
    }


momentum_decay = 0.9
step_rate = 0.5

def orthonormal(factor):
    gram = jnp.einsum('...dr,...ds->...rs', factor, factor, precision=lax.Precision.HIGHEST)
    lower_factor = jnp.linalg.cholesky(gram)
    solved = jax.scipy.linalg.solve_triangular(lower_factor, jnp.swapaxes(factor, -1, -2), lower=True)
    return jnp.swapaxes(solved, -1, -2)

def reference(gradients, errors, warm_right, norm_grads, norm_weights, norm_moment, owners, slot_weights, slot_moment):
    replicas = gradients.shape[0]
    indices = jnp.arange(replicas, dtype=jnp.int32)

    def merged_at(index):
        return gradients[index].astype(jnp.float32) + errors[index]

    def sum_left(right_basis):

        def add_term(total, index):
            term = jnp.einsum('mdk,mkr->mdr', merged_at(index), right_basis, precision=lax.Precision.HIGHEST)
            return (total + term, None)
        start = jnp.zeros((2, DW, RANK), jnp.float32)
        return lax.scan(add_term, start, indices)[0]

    def sum_right(left_basis):

        def add_term(total, index):
            term = jnp.einsum('mdk,mdr->mkr', merged_at(index), left_basis, precision=lax.Precision.HIGHEST)
            return (total + term, None)
        start = jnp.zeros((2, KV, RANK), jnp.float32)
        return lax.scan(add_term, start, indices)[0]
    left_one = orthonormal(sum_left(warm_right))
    right_one = sum_right(left_one) / replicas
    left_two = orthonormal(sum_left(right_one))
    right_two = sum_right(left_two) / replicas
    update = jnp.einsum('mdr,mkr->mdk', left_two, right_two, precision=lax.Precision.HIGHEST)
    new_errors = lax.map(lambda index: merged_at(index) - update, indices)
    summed_norm = jnp.sum(norm_grads, axis=0)
    new_norm_moment = momentum_decay * norm_moment + summed_norm / replicas
    new_norm_weights = norm_weights - step_rate * new_norm_moment
    positions = jnp.arange(PIECES, dtype=jnp.int32)
    same_owner = owners[:, None] == owners[None, :]
    earlier = positions[:, None] < positions[None, :]
    slot_of = jnp.sum((same_owner & earlier).astype(jnp.int32), axis=0).astype(jnp.int32)
    pieces = update.reshape(PIECES, RB, KV)
    fresh = momentum_decay * slot_moment[owners, slot_of] + pieces
    new_slot_moment = slot_moment.at[owners, slot_of].set(fresh)
    rows_new = slot_weights[owners, slot_of].astype(jnp.float32) - step_rate * fresh
    new_weights = rows_new.astype(jnp.bfloat16).reshape(2, DW, KV)
    return (new_errors, new_slot_moment, new_weights, new_norm_weights, new_norm_moment)
```

```python
import functools

import jax
import jax.numpy as jnp
from jax import lax
from jax.experimental import pallas as pl
from jax.experimental.pallas import tpu as pltpu
from jax.sharding import PartitionSpec as P

momentum_decay = 0.9
step_rate = 0.5
MESH = pl.DeviceIdType.MESH
AXES = ("dp", "group")
F32 = jnp.float32
BF16 = jnp.bfloat16
NT = (((1,), (1,)), ((), ()))
NN = (((1,), (0,)), ((), ()))
TN = (((0,), (0,)), ((), ()))
BLOCK = 256


def split(value):
    high = value.astype(BF16)
    return high, (value - high.astype(F32)).astype(BF16)


def bits_of(sizes):
    return [
        [(axis, 1 << b) for b in range(sizes[axis].bit_length() - 1)] for axis in AXES
    ]


def stages_of(sizes, first):
    dp, group = bits_of(sizes)
    near = group + dp[:1]
    rest = dp[1:]
    stages = [near[:1], near[1:]] if first else [near]
    stages += [rest[i : i + 2] for i in range(0, len(rest), 2)]
    return [s for s in stages if s]


def plan_of(stages, tiles):
    plan = []
    held = tiles
    for stage in stages:
        members = 1 << len(stage)
        scatter = held % members == 0
        after = held // members if scatter else held
        plan.append((members, scatter, held, after))
        held = after
    return plan


def peer_of(coords, stage, d):
    out = dict(coords)
    for i, (axis, weight) in enumerate(stage):
        if (d >> i) & 1:
            bit = (coords[axis] // weight) % 2
            out[axis] = out[axis] + weight * (1 - 2 * bit)
    return tuple(out[axis] for axis in AXES)


def place_of(coords, stage, d):
    place = 0
    for i, (axis, weight) in enumerate(stage):
        bit = (coords[axis] // weight) % 2
        if (d >> i) & 1:
            bit = 1 - bit
        place = place + bit * (1 << i)
    return place


def sum_over(coords, stages, plan, part, full, recv, send_sems, recv_sems, works=()):
    works = list(works)
    base = 0
    slot = 0
    sem = 0
    bases = []

    def work():
        if works:
            works.pop(0)()

    for stage, (members, scatter, held, after) in zip(stages, plan):
        copies = []
        bases.append(base)
        for d in range(1, members):
            start = base + place_of(coords, stage, d) * after if scatter else base
            copy = pltpu.make_async_remote_copy(
                src_ref=part.at[pl.ds(start, after)],
                dst_ref=recv.at[pl.ds(slot + (d - 1) * after, after)],
                send_sem=send_sems.at[sem],
                recv_sem=recv_sems.at[sem],
                device_id=peer_of(coords, stage, d),
                device_id_type=MESH,
            )
            copy.start()
            copies.append(copy)
            sem += 1
        work()
        if scatter:
            base = base + place_of(coords, stage, 0) * after
        for copy in copies:
            copy.wait()
        total = part[pl.ds(base, after)]
        for d in range(1, members):
            total = total + recv[pl.ds(slot + (d - 1) * after, after)]
        part[pl.ds(base, after)] = total
        slot += (members - 1) * after
    full[pl.ds(base, after)] = part[pl.ds(base, after)]
    for stage, (members, scatter, held, after), before in reversed(
        list(zip(stages, plan, bases))
    ):
        if not scatter:
            continue
        copies = []
        for d in range(1, members):
            copy = pltpu.make_async_remote_copy(
                src_ref=full.at[pl.ds(base, after)],
                dst_ref=full.at[pl.ds(base, after)],
                send_sem=send_sems.at[sem],
                recv_sem=recv_sems.at[sem],
                device_id=peer_of(coords, stage, d),
                device_id_type=MESH,
            )
            copy.start()
            copies.append(copy)
            sem += 1
        work()
        for copy in copies:
            copy.wait()
        base = before
    while works:
        work()


def tiles_to_wide(tiles, rank):
    per = rank // 8
    count = tiles.shape[0] // per
    blocks = tiles.reshape(count, rank, 128)
    return jnp.concatenate([blocks[i] for i in range(count)], axis=1)


def wide_to_tiles(wide, rank):
    per = rank // 8
    count = wide.shape[1] // 128
    return jnp.concatenate(
        [wide[:, i * 128 : (i + 1) * 128].reshape(per, 8, 128) for i in range(count)],
        axis=0,
    )


def rounds_kernel(
    sizes,
    grads,
    errs,
    warm,
    left_out,
    right_out,
    e_buf,
    g_buf,
    high,
    low,
    l_part_a,
    l_full_a,
    l_recv_a,
    l_part_b,
    l_full_b,
    l_recv_b,
    r_part_a,
    r_full_a,
    r_recv_a,
    r_part_b,
    r_full_b,
    r_recv_b,
    chol,
    load_sems,
    l_send,
    l_got,
    r_send,
    r_got,
):
    replicas = sizes["dp"] * sizes["group"]
    mats, rank, features = warm.shape
    rows = e_buf.shape[0]
    per_mat = rows // mats
    steps = rows // BLOCK
    mat_steps = per_mat // BLOCK
    l_tiles = l_part_a.shape[0]
    r_tiles = r_part_a.shape[0]
    coords = {axis: lax.axis_index(axis) for axis in AXES}
    l_stages, r_stages = stages_of(sizes, True), stages_of(sizes, False)
    l_plan, r_plan = plan_of(l_stages, l_tiles), plan_of(r_stages, r_tiles)

    def load(step):
        span = pl.ds(step * BLOCK, BLOCK)
        return (
            pltpu.make_async_copy(errs.at[span], e_buf.at[span], load_sems.at[0, step]),
            pltpu.make_async_copy(grads.at[span], g_buf.at[span], load_sems.at[1, step]),
        )

    def begin(step, carry):
        for copy in load(step):
            copy.start()
        return carry

    lax.fori_loop(0, steps, begin, 0)

    barrier = pltpu.get_barrier_semaphore()
    seen = []
    for stage in l_stages + r_stages:
        for d in range(1, 1 << len(stage)):
            key = tuple(stage[i] for i in range(len(stage)) if (d >> i) & 1)
            if key not in seen:
                seen.append(key)
                pl.semaphore_signal(
                    barrier,
                    inc=1,
                    device_id=peer_of(coords, stage, d),
                    device_id_type=MESH,
                )
    pl.semaphore_wait(barrier, len(seen))

    tiles_per_block = l_tiles // steps

    def left_block(step, m_high, m_low, right, part):
        stacked, right_high = right
        wide = lax.dot_general(stacked, m_high, NT, preferred_element_type=F32)
        value = wide[:rank] + wide[rank:]
        value = value + lax.dot_general(right_high, m_low, NT, preferred_element_type=F32)
        part[pl.ds(step * tiles_per_block, tiles_per_block)] = wide_to_tiles(value, rank)

    def stack(right):
        right_high, right_low = split(right)
        return jnp.concatenate([right_high, right_low], axis=0), right_high

    for m in range(mats):
        right = stack(warm[m])

        def first(i, carry):
            step = m * mat_steps + i
            span = pl.ds(step * BLOCK, BLOCK)
            for copy in load(step):
                copy.wait()
            merged = g_buf[span].astype(F32) + e_buf[span]
            m_high, m_low = split(merged)
            high[span] = m_high
            low[span] = m_low
            left_block(step, m_high, m_low, right, l_part_a)
            return carry

        lax.fori_loop(0, mat_steps, first, 0)

    def left_product(rights, part):
        for m in range(mats):
            right = stack(rights[m])

            def one(i, carry):
                step = m * mat_steps + i
                span = pl.ds(step * BLOCK, BLOCK)
                left_block(step, high[span], low[span], right, part)
                return carry

            lax.fori_loop(0, mat_steps, one, 0)

    mat_r_tiles = r_tiles // mats

    def right_product(full, part):
        for m in range(mats):

            def one(i, total):
                step = m * mat_steps + i
                span = pl.ds(step * BLOCK, BLOCK)
                left = tiles_to_wide(full[pl.ds(step * tiles_per_block, tiles_per_block)], rank)
                stacked, left_high = stack(left)
                wide = lax.dot_general(stacked, high[span], NN, preferred_element_type=F32)
                more = lax.dot_general(left_high, low[span], NN, preferred_element_type=F32)
                return total + (wide[:rank] + wide[rank:] + more)

            total = lax.fori_loop(0, mat_steps, one, jnp.zeros((rank, features), F32))
            part[m * mat_r_tiles : (m + 1) * mat_r_tiles] = wide_to_tiles(total, rank)

    row_index = lax.broadcasted_iota(jnp.int32, (rank, 128), 0)
    lane_index = lax.broadcasted_iota(jnp.int32, (rank, 128), 1)

    def gram(full):
        for m in range(mats):

            def one(i, total):
                step = m * mat_steps + i
                left = tiles_to_wide(full[pl.ds(step * tiles_per_block, tiles_per_block)], rank)
                return total + lax.dot_general(
                    left, left, NT, precision=lax.Precision.HIGHEST, preferred_element_type=F32
                )

            total = lax.fori_loop(0, mat_steps, one, jnp.zeros((rank, rank), F32))
            unit = (lane_index == row_index + rank).astype(F32)
            chol[m] = unit + jnp.concatenate(
                [total, jnp.zeros((rank, 128 - rank), F32)], axis=1
            )

    def eliminate(k, carry):
        out = []
        for value in carry:
            row = jnp.sum(jnp.where(row_index == k, value, 0.0), axis=0, keepdims=True)
            column = jnp.sum(jnp.where(lane_index == k, value, 0.0), axis=1, keepdims=True)
            pivot = jnp.sum(jnp.where(lane_index[:1] == k, row, 0.0), axis=1, keepdims=True)
            factor = jnp.where(row_index > k, column / pivot, 0.0)
            out.append(value - factor * row)
        return tuple(out)

    def eliminate_some(lower, upper):
        values = lax.fori_loop(
            lower, upper, eliminate, tuple(chol[m] for m in range(mats))
        )
        for m in range(mats):
            chol[m] = values[m]

    def inverse_factor(m):
        value = chol[m]
        pivots = jnp.sum(jnp.where(lane_index == row_index, value, 0.0), axis=1, keepdims=True)
        return value[:, rank : 2 * rank] * lax.rsqrt(pivots)

    def works_of(full):
        quarter = rank // 4

        def opening():
            gram(full)
            eliminate_some(0, quarter)

        return [opening] + [
            functools.partial(eliminate_some, i * quarter, (i + 1) * quarter)
            for i in range(1, 4)
        ]

    def exact(a, b, dims):
        return lax.dot_general(
            a, b, dims, precision=lax.Precision.HIGHEST, preferred_element_type=F32
        )

    def right_sum(full, m):
        return tiles_to_wide(full[m * mat_r_tiles : (m + 1) * mat_r_tiles], rank)

    sum_over(coords, l_stages, l_plan, l_part_a, l_full_a, l_recv_a, l_send.at[0], l_got.at[0])
    right_product(l_full_a, r_part_a)
    sum_over(
        coords, r_stages, r_plan, r_part_a, r_full_a, r_recv_a, r_send.at[0], r_got.at[0],
        works_of(l_full_a),
    )
    rights = [
        exact(inverse_factor(m), right_sum(r_full_a, m), NN) / replicas for m in range(mats)
    ]
    left_product(rights, l_part_b)
    sum_over(coords, l_stages, l_plan, l_part_b, l_full_b, l_recv_b, l_send.at[1], l_got.at[1])
    right_product(l_full_b, r_part_b)
    sum_over(
        coords, r_stages, r_plan, r_part_b, r_full_b, r_recv_b, r_send.at[1], r_got.at[1],
        works_of(l_full_b),
    )
    for m in range(mats):
        inverse = inverse_factor(m)
        right_two = exact(inverse, right_sum(r_full_b, m), NN) / replicas
        right_out[m] = right_two
        for i in range(mat_steps):
            step = m * mat_steps + i
            left = tiles_to_wide(
                l_full_b[step * tiles_per_block : (step + 1) * tiles_per_block], rank
            )
            left_out[m, :, i * BLOCK : (i + 1) * BLOCK] = exact(inverse, left, NN)


def rounds(sizes, grads, errs, warm):
    rows, features = errs.shape
    mats, rank, _ = warm.shape
    l_tiles = rows * rank // 1024
    r_tiles = mats * features * rank // 1024
    l_plan = plan_of(stages_of(sizes, True), l_tiles)
    r_plan = plan_of(stages_of(sizes, False), r_tiles)

    def slots(plan):
        return sum((members - 1) * after for members, _, _, after in plan)

    def sems(plan):
        return sum((members - 1) * (2 if scatter else 1) for members, scatter, _, _ in plan)

    def tiles(count):
        return pltpu.VMEM((count, 8, 128), F32)

    l_bufs = [tiles(l_tiles), tiles(l_tiles), tiles(slots(l_plan))]
    r_bufs = [tiles(r_tiles), tiles(r_tiles), tiles(slots(r_plan))]
    return pl.pallas_call(
        functools.partial(rounds_kernel, sizes),
        out_shape=(
            jax.ShapeDtypeStruct((mats, rank, rows // mats), F32),
            jax.ShapeDtypeStruct((mats, rank, features), F32),
        ),
        in_specs=[
            pl.BlockSpec(memory_space=pl.ANY),
            pl.BlockSpec(memory_space=pl.ANY),
            pl.BlockSpec(memory_space=pltpu.VMEM),
        ],
        out_specs=(
            pl.BlockSpec(memory_space=pltpu.VMEM),
            pl.BlockSpec(memory_space=pltpu.VMEM),
        ),
        scratch_shapes=[
            pltpu.VMEM((rows, features), F32),
            pltpu.VMEM((rows, features), BF16),
            pltpu.VMEM((rows, features), BF16),
            pltpu.VMEM((rows, features), BF16),
            *l_bufs,
            *l_bufs,
            *r_bufs,
            *r_bufs,
            pltpu.VMEM((mats, rank, 128), F32),
            pltpu.SemaphoreType.DMA((2, rows // BLOCK)),
            pltpu.SemaphoreType.DMA((2, sems(l_plan))),
            pltpu.SemaphoreType.DMA((2, sems(l_plan))),
            pltpu.SemaphoreType.DMA((2, sems(r_plan))),
            pltpu.SemaphoreType.DMA((2, sems(r_plan))),
        ],
        compiler_params=pltpu.CompilerParams(
            collective_id=0, has_side_effects=True, vmem_limit_bytes=44 * 1024 * 1024
        ),
        name="rounds",
    )(grads, errs, warm)


def finish_kernel(per, slots, places, mine, *refs):
    left, right, grads, errs, moment = refs[:5]
    bases = refs[5 : 5 + per]
    new_errs, weights, new_moment = refs[5 + per :]
    step = pl.program_id(0)
    piece_rows = moment.shape[1]

    @pl.when(step == 0)
    def _():
        new_moment[...] = moment[...]

    l_high, l_low = split(left[0])
    r_high, r_low = split(right[0])
    update = lax.dot_general(
        jnp.concatenate([l_high, l_low, l_high], axis=0),
        jnp.concatenate([r_high, r_high, r_low], axis=0),
        TN,
        preferred_element_type=F32,
    )
    new_errs[...] = (grads[...].astype(F32) + errs[...]) - update
    for i in range(per):
        rows = slice(i * piece_rows, (i + 1) * piece_rows)
        weights[rows] = (bases[i][0] - step_rate * update[rows]).astype(BF16)
        for s in range(slots):

            @pl.when(mine[s] == step * per + i)
            def _():
                new_moment[s] = momentum_decay * moment[s] + update[rows]


def finish(left, right, grads, errs, moment, gathered, places, mine):
    rows, features = errs.shape
    mats, rank, mat_rows = left.shape
    slots, piece_rows, _ = moment.shape
    block = max(BLOCK, piece_rows)
    per = block // piece_rows
    mat_steps = mat_rows // block

    def by_piece(i):
        return pl.BlockSpec(
            (1, piece_rows, features), lambda g, places, mine: (places[g * per + i], 0, 0)
        )

    rows_spec = pl.BlockSpec((block, features), lambda g, places, mine: (g, 0))
    slot_spec = pl.BlockSpec((slots, piece_rows, features), lambda g, places, mine: (0, 0, 0))
    return pl.pallas_call(
        functools.partial(finish_kernel, per, slots),
        out_shape=(
            jax.ShapeDtypeStruct((rows, features), F32),
            jax.ShapeDtypeStruct((rows, features), BF16),
            jax.ShapeDtypeStruct(moment.shape, F32),
        ),
        grid_spec=pltpu.PrefetchScalarGridSpec(
            num_scalar_prefetch=2,
            grid=(rows // block,),
            in_specs=[
                pl.BlockSpec(
                    (1, rank, block),
                    lambda g, places, mine: (g // mat_steps, 0, g % mat_steps),
                ),
                pl.BlockSpec(
                    (1, rank, features), lambda g, places, mine: (g // mat_steps, 0, 0)
                ),
                rows_spec,
                rows_spec,
                slot_spec,
                *[by_piece(i) for i in range(per)],
            ],
            out_specs=(rows_spec, rows_spec, slot_spec),
        ),
        compiler_params=pltpu.CompilerParams(vmem_limit_bytes=40 * 1024 * 1024),
        name="finish",
    )(places, mine, left, right, grads, errs, moment, *([gathered] * per))


def on_device(
    sizes,
    gradients,
    errors,
    warm_right,
    norm_grads,
    norm_weights,
    norm_moment,
    owners,
    slot_weights,
    slot_moment,
):
    replicas = sizes["dp"] * sizes["group"]
    mats, mat_rows, features = gradients.shape[1:]
    slots, piece_rows = slot_moment.shape[1:3]
    piece_count = owners.shape[0]
    base = slot_weights[0].astype(F32) - (step_rate * momentum_decay) * slot_moment[0]
    gathered = lax.all_gather(base, AXES, axis=0, tiled=True)
    norms = lax.all_gather(norm_grads[0].reshape(-1, 128), AXES, axis=0)
    norm_sum = jnp.sum(norms, axis=0).reshape(norm_moment.shape)
    new_norm_moment = momentum_decay * norm_moment + norm_sum / replicas
    new_norm_weights = norm_weights - step_rate * new_norm_moment

    positions = jnp.arange(piece_count, dtype=jnp.int32)
    same_owner = owners[:, None] == owners[None, :]
    earlier = positions[:, None] < positions[None, :]
    slot_of = jnp.sum((same_owner & earlier).astype(jnp.int32), axis=0)
    places = owners * slots + slot_of
    own_places = lax.axis_index(AXES) * slots + jnp.arange(slots, dtype=jnp.int32)
    here = own_places[:, None] == places[None, :]
    mine = jnp.max(jnp.where(here, positions[None, :], -1), axis=1)

    grads = gradients.reshape(mats * mat_rows, features)
    errs = errors.reshape(mats * mat_rows, features)
    left_two, right_two = rounds(sizes, grads, errs, jnp.swapaxes(warm_right, 1, 2))
    new_errors, new_weights, new_moment = finish(
        left_two, right_two, grads, errs, slot_moment[0], gathered, places, mine
    )
    return (
        new_errors.reshape(errors.shape),
        new_moment[None],
        new_weights.reshape(mats, mat_rows, features),
        new_norm_weights,
        new_norm_moment,
    )


def solution(mesh):
    placed = (
        P(AXES, None, None, None),
        P(AXES, None, None, None),
        P(),
        P(AXES, None, None),
        P(),
        P(),
        P(),
        P(AXES, None, None, None),
        P(AXES, None, None, None),
    )
    return jax.shard_map(
        functools.partial(on_device, dict(mesh.shape)),
        mesh=mesh,
        in_specs=placed,
        out_specs=(
            P(AXES, None, None, None),
            P(AXES, None, None, None),
            P(),
            P(),
            P(),
        ),
        check_vma=False,
    )
```

```python
import functools

import jax
import jax.numpy as jnp
from jax import lax
from jax.experimental import pallas as pl
from jax.experimental.pallas import tpu as pltpu
from jax.sharding import PartitionSpec as P

momentum_decay = 0.9
step_rate = 0.5
MESH = pl.DeviceIdType.MESH
AXES = ("dp", "group")
F32 = jnp.float32
BF16 = jnp.bfloat16
NT = (((1,), (1,)), ((), ()))
NN = (((1,), (0,)), ((), ()))
TN = (((0,), (0,)), ((), ()))
BLOCK = 256


def split(value):
    high = value.astype(BF16)
    return high, (value - high.astype(F32)).astype(BF16)


def bits_of(sizes):
    return [
        [(axis, 1 << b) for b in range(sizes[axis].bit_length() - 1)] for axis in AXES
    ]


def stages_of(sizes, first):
    dp, group = bits_of(sizes)
    near = group + dp[:1]
    rest = dp[1:]
    stages = [near[:1], near[1:]] if first else [near]
    stages += [rest[i : i + 2] for i in range(0, len(rest), 2)]
    return [s for s in stages if s]


def plan_of(stages, tiles):
    plan = []
    held = tiles
    for stage in stages:
        members = 1 << len(stage)
        scatter = held % members == 0
        after = held // members if scatter else held
        plan.append((members, scatter, held, after))
        held = after
    return plan


def peer_of(coords, stage, d):
    out = dict(coords)
    for i, (axis, weight) in enumerate(stage):
        if (d >> i) & 1:
            bit = (coords[axis] // weight) % 2
            out[axis] = out[axis] + weight * (1 - 2 * bit)
    return tuple(out[axis] for axis in AXES)


def place_of(coords, stage, d):
    place = 0
    for i, (axis, weight) in enumerate(stage):
        bit = (coords[axis] // weight) % 2
        if (d >> i) & 1:
            bit = 1 - bit
        place = place + bit * (1 << i)
    return place


def sum_over(coords, stages, plan, part, full, recv, send_sems, recv_sems, works=()):
    works = list(works)
    base = 0
    slot = 0
    sem = 0
    bases = []

    def work():
        if works:
            works.pop(0)()

    for stage, (members, scatter, held, after) in zip(stages, plan):
        copies = []
        bases.append(base)
        for d in range(1, members):
            start = base + place_of(coords, stage, d) * after if scatter else base
            copy = pltpu.make_async_remote_copy(
                src_ref=part.at[pl.ds(start, after)],
                dst_ref=recv.at[pl.ds(slot + (d - 1) * after, after)],
                send_sem=send_sems.at[sem],
                recv_sem=recv_sems.at[sem],
                device_id=peer_of(coords, stage, d),
                device_id_type=MESH,
            )
            copy.start()
            copies.append(copy)
            sem += 1
        work()
        if scatter:
            base = base + place_of(coords, stage, 0) * after
        for copy in copies:
            copy.wait()
        total = part[pl.ds(base, after)]
        for d in range(1, members):
            total = total + recv[pl.ds(slot + (d - 1) * after, after)]
        part[pl.ds(base, after)] = total
        slot += (members - 1) * after
    full[pl.ds(base, after)] = part[pl.ds(base, after)]
    for stage, (members, scatter, held, after), before in reversed(
        list(zip(stages, plan, bases))
    ):
        if not scatter:
            continue
        copies = []
        for d in range(1, members):
            copy = pltpu.make_async_remote_copy(
                src_ref=full.at[pl.ds(base, after)],
                dst_ref=full.at[pl.ds(base, after)],
                send_sem=send_sems.at[sem],
                recv_sem=recv_sems.at[sem],
                device_id=peer_of(coords, stage, d),
                device_id_type=MESH,
            )
            copy.start()
            copies.append(copy)
            sem += 1
        work()
        for copy in copies:
            copy.wait()
        base = before
    while works:
        work()


def tiles_to_wide(tiles, rank):
    per = rank // 8
    count = tiles.shape[0] // per
    blocks = tiles.reshape(count, rank, 128)
    return jnp.concatenate([blocks[i] for i in range(count)], axis=1)


def wide_to_tiles(wide, rank):
    per = rank // 8
    count = wide.shape[1] // 128
    return jnp.concatenate(
        [wide[:, i * 128 : (i + 1) * 128].reshape(per, 8, 128) for i in range(count)],
        axis=0,
    )


def rounds_kernel(
    sizes,
    grads,
    errs,
    warm,
    norms,
    left_out,
    right_out,
    norm_out,
    e_buf,
    g_buf,
    high,
    low,
    l_part_a,
    l_full_a,
    l_recv_a,
    l_part_b,
    l_full_b,
    l_recv_b,
    r_part_a,
    r_full_a,
    r_recv_a,
    r_part_b,
    r_full_b,
    r_recv_b,
    chol,
    load_sems,
    l_send,
    l_got,
    r_send,
    r_got,
):
    replicas = sizes["dp"] * sizes["group"]
    mats, rank, features = warm.shape
    rows = e_buf.shape[0]
    per_mat = rows // mats
    steps = rows // BLOCK
    mat_steps = per_mat // BLOCK
    l_tiles = l_part_a.shape[0]
    sum_tiles = r_part_a.shape[0]
    r_tiles = mats * features * rank // 1024
    norm_tiles = norms.shape[0]
    coords = {axis: lax.axis_index(axis) for axis in AXES}
    l_stages, r_stages = stages_of(sizes, True), stages_of(sizes, False)
    l_plan, r_plan = plan_of(l_stages, l_tiles), plan_of(r_stages, sum_tiles)

    def load(step):
        span = pl.ds(step * BLOCK, BLOCK)
        return (
            pltpu.make_async_copy(errs.at[span], e_buf.at[span], load_sems.at[0, step]),
            pltpu.make_async_copy(grads.at[span], g_buf.at[span], load_sems.at[1, step]),
        )

    def begin(step, carry):
        for copy in load(step):
            copy.start()
        return carry

    lax.fori_loop(0, steps, begin, 0)

    barrier = pltpu.get_barrier_semaphore()
    seen = []
    for stage in l_stages + r_stages:
        for d in range(1, 1 << len(stage)):
            key = tuple(stage[i] for i in range(len(stage)) if (d >> i) & 1)
            if key not in seen:
                seen.append(key)
                pl.semaphore_signal(
                    barrier,
                    inc=1,
                    device_id=peer_of(coords, stage, d),
                    device_id_type=MESH,
                )
    pl.semaphore_wait(barrier, len(seen))

    for part in (r_part_a, r_part_b):
        part[r_tiles : r_tiles + norm_tiles] = norms[...]
        if sum_tiles > r_tiles + norm_tiles:
            left_over = sum_tiles - r_tiles - norm_tiles
            part[r_tiles + norm_tiles :] = jnp.zeros((left_over, 8, 128), F32)

    tiles_per_block = l_tiles // steps

    def left_block(step, m_high, m_low, right, part):
        stacked, right_high = right
        wide = lax.dot_general(stacked, m_high, NT, preferred_element_type=F32)
        value = wide[:rank] + wide[rank:]
        value = value + lax.dot_general(right_high, m_low, NT, preferred_element_type=F32)
        part[pl.ds(step * tiles_per_block, tiles_per_block)] = wide_to_tiles(value, rank)

    def stack(right):
        right_high, right_low = split(right)
        return jnp.concatenate([right_high, right_low], axis=0), right_high

    for m in range(mats):
        right = stack(warm[m])

        def first(i, carry):
            step = m * mat_steps + i
            span = pl.ds(step * BLOCK, BLOCK)
            for copy in load(step):
                copy.wait()
            merged = g_buf[span].astype(F32) + e_buf[span]
            m_high, m_low = split(merged)
            high[span] = m_high
            low[span] = m_low
            left_block(step, m_high, m_low, right, l_part_a)
            return carry

        lax.fori_loop(0, mat_steps, first, 0)

    def left_product(rights, part):
        for m in range(mats):
            right = stack(rights[m])

            def one(i, carry):
                step = m * mat_steps + i
                span = pl.ds(step * BLOCK, BLOCK)
                left_block(step, high[span], low[span], right, part)
                return carry

            lax.fori_loop(0, mat_steps, one, 0)

    mat_r_tiles = r_tiles // mats

    def right_product(full, part):
        for m in range(mats):

            def one(i, total):
                step = m * mat_steps + i
                span = pl.ds(step * BLOCK, BLOCK)
                left = tiles_to_wide(full[pl.ds(step * tiles_per_block, tiles_per_block)], rank)
                stacked, left_high = stack(left)
                wide = lax.dot_general(stacked, high[span], NN, preferred_element_type=F32)
                more = lax.dot_general(left_high, low[span], NN, preferred_element_type=F32)
                return total + (wide[:rank] + wide[rank:] + more)

            total = lax.fori_loop(0, mat_steps, one, jnp.zeros((rank, features), F32))
            part[m * mat_r_tiles : (m + 1) * mat_r_tiles] = wide_to_tiles(total, rank)

    row_index = lax.broadcasted_iota(jnp.int32, (rank, 128), 0)
    lane_index = lax.broadcasted_iota(jnp.int32, (rank, 128), 1)

    def gram(full):
        for m in range(mats):

            def one(i, total):
                step = m * mat_steps + i
                left = tiles_to_wide(full[pl.ds(step * tiles_per_block, tiles_per_block)], rank)
                return total + lax.dot_general(
                    left, left, NT, precision=lax.Precision.HIGHEST, preferred_element_type=F32
                )

            total = lax.fori_loop(0, mat_steps, one, jnp.zeros((rank, rank), F32))
            unit = (lane_index == row_index + rank).astype(F32)
            chol[m] = unit + jnp.concatenate(
                [total, jnp.zeros((rank, 128 - rank), F32)], axis=1
            )

    def eliminate(k, carry):
        out = []
        for value in carry:
            row = jnp.sum(jnp.where(row_index == k, value, 0.0), axis=0, keepdims=True)
            column = jnp.sum(jnp.where(lane_index == k, value, 0.0), axis=1, keepdims=True)
            pivot = jnp.sum(jnp.where(lane_index[:1] == k, row, 0.0), axis=1, keepdims=True)
            factor = jnp.where(row_index > k, column / pivot, 0.0)
            out.append(value - factor * row)
        return tuple(out)

    def eliminate_some(lower, upper):
        values = lax.fori_loop(
            lower, upper, eliminate, tuple(chol[m] for m in range(mats))
        )
        for m in range(mats):
            chol[m] = values[m]

    def inverse_factor(m):
        value = chol[m]
        pivots = jnp.sum(jnp.where(lane_index == row_index, value, 0.0), axis=1, keepdims=True)
        return value[:, rank : 2 * rank] * lax.rsqrt(pivots)

    def works_of(full):
        quarter = rank // 4

        def opening():
            gram(full)
            eliminate_some(0, quarter)

        return [opening] + [
            functools.partial(eliminate_some, i * quarter, (i + 1) * quarter)
            for i in range(1, 4)
        ]

    def exact(a, b, dims):
        return lax.dot_general(
            a, b, dims, precision=lax.Precision.HIGHEST, preferred_element_type=F32
        )

    def right_sum(full, m):
        return tiles_to_wide(full[m * mat_r_tiles : (m + 1) * mat_r_tiles], rank)

    sum_over(coords, l_stages, l_plan, l_part_a, l_full_a, l_recv_a, l_send.at[0], l_got.at[0])
    right_product(l_full_a, r_part_a)
    sum_over(
        coords, r_stages, r_plan, r_part_a, r_full_a, r_recv_a, r_send.at[0], r_got.at[0],
        works_of(l_full_a),
    )
    rights = [
        exact(inverse_factor(m), right_sum(r_full_a, m), NN) / replicas for m in range(mats)
    ]
    left_product(rights, l_part_b)
    sum_over(coords, l_stages, l_plan, l_part_b, l_full_b, l_recv_b, l_send.at[1], l_got.at[1])
    right_product(l_full_b, r_part_b)
    sum_over(
        coords, r_stages, r_plan, r_part_b, r_full_b, r_recv_b, r_send.at[1], r_got.at[1],
        works_of(l_full_b),
    )
    norm_out[...] = r_full_a[r_tiles : r_tiles + norm_tiles]
    for m in range(mats):
        inverse = inverse_factor(m)
        right_two = exact(inverse, right_sum(r_full_b, m), NN) / replicas
        right_out[m] = right_two
        for i in range(mat_steps):
            step = m * mat_steps + i
            left = tiles_to_wide(
                l_full_b[step * tiles_per_block : (step + 1) * tiles_per_block], rank
            )
            left_out[m, :, i * BLOCK : (i + 1) * BLOCK] = exact(inverse, left, NN)


def rounds(sizes, grads, errs, warm, norms):
    rows, features = errs.shape
    mats, rank, _ = warm.shape
    l_tiles = rows * rank // 1024
    r_tiles = mats * features * rank // 1024 + norms.shape[0]
    r_tiles = (r_tiles + 7) // 8 * 8
    l_plan = plan_of(stages_of(sizes, True), l_tiles)
    r_plan = plan_of(stages_of(sizes, False), r_tiles)

    def slots(plan):
        return sum((members - 1) * after for members, _, _, after in plan)

    def sems(plan):
        return sum((members - 1) * (2 if scatter else 1) for members, scatter, _, _ in plan)

    def tiles(count):
        return pltpu.VMEM((count, 8, 128), F32)

    l_bufs = [tiles(l_tiles), tiles(l_tiles), tiles(slots(l_plan))]
    r_bufs = [tiles(r_tiles), tiles(r_tiles), tiles(slots(r_plan))]
    return pl.pallas_call(
        functools.partial(rounds_kernel, sizes),
        out_shape=(
            jax.ShapeDtypeStruct((mats, rank, rows // mats), F32),
            jax.ShapeDtypeStruct((mats, rank, features), F32),
            jax.ShapeDtypeStruct(norms.shape, F32),
        ),
        in_specs=[
            pl.BlockSpec(memory_space=pl.ANY),
            pl.BlockSpec(memory_space=pl.ANY),
            pl.BlockSpec(memory_space=pltpu.VMEM),
            pl.BlockSpec(memory_space=pltpu.VMEM),
        ],
        out_specs=(
            pl.BlockSpec(memory_space=pltpu.VMEM),
            pl.BlockSpec(memory_space=pltpu.VMEM),
            pl.BlockSpec(memory_space=pltpu.VMEM),
        ),
        scratch_shapes=[
            pltpu.VMEM((rows, features), F32),
            pltpu.VMEM((rows, features), BF16),
            pltpu.VMEM((rows, features), BF16),
            pltpu.VMEM((rows, features), BF16),
            *l_bufs,
            *l_bufs,
            *r_bufs,
            *r_bufs,
            pltpu.VMEM((mats, rank, 128), F32),
            pltpu.SemaphoreType.DMA((2, rows // BLOCK)),
            pltpu.SemaphoreType.DMA((2, sems(l_plan))),
            pltpu.SemaphoreType.DMA((2, sems(l_plan))),
            pltpu.SemaphoreType.DMA((2, sems(r_plan))),
            pltpu.SemaphoreType.DMA((2, sems(r_plan))),
        ],
        compiler_params=pltpu.CompilerParams(
            collective_id=0, has_side_effects=True, vmem_limit_bytes=56 * 1024 * 1024
        ),
        name="rounds",
    )(grads, errs, warm, norms)


def finish_kernel(per, slots, places, mine, *refs):
    left, right, grads, errs, moment = refs[:5]
    bases = refs[5 : 5 + per]
    new_errs, weights, new_moment = refs[5 + per :]
    step = pl.program_id(0)
    piece_rows = moment.shape[1]

    @pl.when(step == 0)
    def _():
        new_moment[...] = moment[...]

    l_high, l_low = split(left[0])
    r_high, r_low = split(right[0])
    update = lax.dot_general(
        jnp.concatenate([l_high, l_low, l_high], axis=0),
        jnp.concatenate([r_high, r_high, r_low], axis=0),
        TN,
        preferred_element_type=F32,
    )
    new_errs[...] = (grads[...].astype(F32) + errs[...]) - update
    for i in range(per):
        rows = slice(i * piece_rows, (i + 1) * piece_rows)
        weights[rows] = (bases[i][0] - step_rate * update[rows]).astype(BF16)
        for s in range(slots):

            @pl.when(mine[s] == step * per + i)
            def _():
                new_moment[s] = momentum_decay * moment[s] + update[rows]


def finish(left, right, grads, errs, moment, gathered, places, mine):
    rows, features = errs.shape
    mats, rank, mat_rows = left.shape
    slots, piece_rows, _ = moment.shape
    block = max(2 * BLOCK, piece_rows)
    per = block // piece_rows
    mat_steps = mat_rows // block

    def by_piece(i):
        return pl.BlockSpec(
            (1, piece_rows, features), lambda g, places, mine: (places[g * per + i], 0, 0)
        )

    rows_spec = pl.BlockSpec((block, features), lambda g, places, mine: (g, 0))
    slot_spec = pl.BlockSpec((slots, piece_rows, features), lambda g, places, mine: (0, 0, 0))
    return pl.pallas_call(
        functools.partial(finish_kernel, per, slots),
        out_shape=(
            jax.ShapeDtypeStruct((rows, features), F32),
            jax.ShapeDtypeStruct((rows, features), BF16),
            jax.ShapeDtypeStruct(moment.shape, F32),
        ),
        grid_spec=pltpu.PrefetchScalarGridSpec(
            num_scalar_prefetch=2,
            grid=(rows // block,),
            in_specs=[
                pl.BlockSpec(
                    (1, rank, block),
                    lambda g, places, mine: (g // mat_steps, 0, g % mat_steps),
                ),
                pl.BlockSpec(
                    (1, rank, features), lambda g, places, mine: (g // mat_steps, 0, 0)
                ),
                rows_spec,
                rows_spec,
                slot_spec,
                *[by_piece(i) for i in range(per)],
            ],
            out_specs=(rows_spec, rows_spec, slot_spec),
        ),
        compiler_params=pltpu.CompilerParams(vmem_limit_bytes=58 * 1024 * 1024),
        name="finish",
    )(places, mine, left, right, grads, errs, moment, *([gathered] * per))


def on_device(
    sizes,
    gradients,
    errors,
    warm_right,
    norm_grads,
    norm_weights,
    norm_moment,
    owners,
    slot_weights,
    slot_moment,
):
    replicas = sizes["dp"] * sizes["group"]
    mats, mat_rows, features = gradients.shape[1:]
    slots, piece_rows = slot_moment.shape[1:3]
    piece_count = owners.shape[0]
    base = slot_weights[0].astype(F32) - (step_rate * momentum_decay) * slot_moment[0]
    gathered = lax.all_gather(base[None], AXES, axis=0, tiled=True)
    gathered = gathered.reshape(replicas * slots, piece_rows, features)

    positions = jnp.arange(piece_count, dtype=jnp.int32)
    same_owner = owners[:, None] == owners[None, :]
    earlier = positions[:, None] < positions[None, :]
    slot_of = jnp.sum((same_owner & earlier).astype(jnp.int32), axis=0)
    places = owners * slots + slot_of
    own_places = lax.axis_index(AXES) * slots + jnp.arange(slots, dtype=jnp.int32)
    here = own_places[:, None] == places[None, :]
    mine = jnp.max(jnp.where(here, positions[None, :], -1), axis=1)

    grads = gradients.reshape(mats * mat_rows, features)
    errs = errors.reshape(mats * mat_rows, features)
    left_two, right_two, norm_sum = rounds(
        sizes, grads, errs, jnp.swapaxes(warm_right, 1, 2), norm_grads.reshape(-1, 8, 128)
    )
    norm_sum = norm_sum.reshape(norm_moment.shape)
    new_norm_moment = momentum_decay * norm_moment + norm_sum / replicas
    new_norm_weights = norm_weights - step_rate * new_norm_moment
    new_errors, new_weights, new_moment = finish(
        left_two, right_two, grads, errs, slot_moment[0], gathered, places, mine
    )
    return (
        new_errors.reshape(errors.shape),
        new_moment[None],
        new_weights.reshape(mats, mat_rows, features),
        new_norm_weights,
        new_norm_moment,
    )


def solution(mesh):
    placed = (
        P(AXES, None, None, None),
        P(AXES, None, None, None),
        P(),
        P(AXES, None, None),
        P(),
        P(),
        P(),
        P(AXES, None, None, None),
        P(AXES, None, None, None),
    )
    return jax.shard_map(
        functools.partial(on_device, dict(mesh.shape)),
        mesh=mesh,
        in_specs=placed,
        out_specs=(
            P(AXES, None, None, None),
            P(AXES, None, None, None),
            P(),
            P(),
            P(),
        ),
        check_vma=False,
    )
```
